512 devices in a mesh: shot: 16 (over z_lo, core), px: 8 (over y, z_hi), py: 4 (over x).
Axes of the slice: x: 4, y: 4, z: 16 (z_hi: 2, z_lo: 8; z = z_hi * 8 + z_lo), core: 2. Of those that a mesh axis runs over, the one named last changes fastest.
Arguments:
- fwd_before: float32 [16, 32, 192, 512], P('shot', None, 'px', 'py'), may hold values from -6 to 6
- fwd_now: float32 [16, 32, 192, 512], P('shot', None, 'px', 'py'), may hold values from -6 to 6
- adj_after: float32 [16, 32, 192, 512], P('shot', None, 'px', 'py'), may hold values from -6 to 6
- adj_now: float32 [16, 32, 192, 512], P('shot', None, 'px', 'py'), may hold values from -8 to 8
- speed: float32 [32, 192, 512], P(None, 'px', 'py'), may hold values from 1.5 to 4.5
- src_pos: int32 [16, 8, 3], P('shot'), may hold values from 0 to 511, as said below
- src_amp: float32 [16, 2, 8], P('shot'), may hold values from -12 to 12
- rec_pos: int32 [16, 256, 3], P('shot'), may hold values from 0 to 511, as said below
- observed: float32 [16, 2, 256], P('shot'), may hold values from -6 to 6
- rate: float32 [1], replicated, may hold values from 0.05 to 0.2
Outputs:
- fwd_mid: float32 [16, 32, 192, 512], P('shot', None, 'px', 'py')
- fwd_last: float32 [16, 32, 192, 512], P('shot', None, 'px', 'py')
- adj_mid: float32 [16, 32, 192, 512], P('shot', None, 'px', 'py')
- adj_last: float32 [16, 32, 192, 512], P('shot', None, 'px', 'py')
- new_speed: float32 [32, 192, 512], P(None, 'px', 'py')
- gradient: float32 [32, 192, 512], P('shot', 'px', 'py')
The draws below stay inside these ranges and needn't reach their ends.
Inputs may be any that keep to these rules, and one draw needn't show every extreme that they name: `src_pos`: each row holds a depth index below 32, a first index below 192 and a second index below 512; cells may repeat. `rec_pos`: each row holds a depth index below 32, a first index below 192 and a second index below 512; cells may repeat.
All inputs are finite; a program needn't handle non-finite values.
Results may differ from the reference program's by a relative error of at most 0.00002.
Values sent between devices are 32-bit elements; how exact they have to be, the bound alone decides.
A program may use at most 64 MiB of HBM per device.

```python
import math
import jax
import jax.numpy as jnp
from jax import lax

NZ = 32
NSRC = 8
NREC = 256
NSHOT = 16
NX = 192
NY = 512


def grid_points(key, count):
    key_depth, key_first, key_second = jax.random.split(key, 3)
    depth = jax.random.randint(key_depth, (NSHOT, count), 0, NZ)
    first = jax.random.randint(key_first, (NSHOT, count), 0, NX)
    second = jax.random.randint(key_second, (NSHOT, count), 0, NY)
    second = second.at[:, 0].set(NY - 1)
    depth = depth.at[:, 1].set(0)
    return jnp.stack([depth, first, second], axis=-1).astype(jnp.int32)


def draw_src_pos(key, part):
    key = jax.random.fold_in(key, 1)
    return grid_points(key, NSRC)


def draw_rec_pos(key, part):
    key = jax.random.fold_in(key, 2)
    return grid_points(key, NREC)


def spiked(drawn, stream_key, source, target, blocks, factor):
    owner, partner = [(jnp.arange(drawn.shape[position]) // (drawn.shape[position] // blocks)).reshape([-1 if axis == position else 1 for axis in range(drawn.ndim)]) for position in (source, target)]
    chosen = jax.random.permutation(stream_key, blocks)[partner]
    strong = (owner == chosen) | (owner == (partner + blocks // 2) % blocks)
    return jnp.where(strong, factor * drawn, drawn)


def block_scale(stream_key, shape, pieces, low, largest):
    def one(dim, blocks):
        heights = jax.random.uniform(jax.random.fold_in(jax.random.fold_in(stream_key, 6), dim), (blocks,), jnp.float32, low / len(pieces), largest / len(pieces))
        return jnp.repeat(jnp.exp(heights), shape[dim] // blocks).reshape((-1,) + (1,) * (len(shape) - dim - 1))

    level = one(*pieces[0])
    for cut in pieces[1:]:
        level = level * one(*cut)
    return level


def bell_draw(own_key, extent, scale, most, cuts=(), dtype=jnp.bfloat16):
    result = scale * jax.random.normal(own_key, extent, jnp.float32)
    if cuts:
        result = result * block_scale(own_key, extent, cuts, -0.22, 0.18)
    return jnp.clip(result, -most, most).astype(dtype)


def noise_with(key, extent, deviation, bound, pieces, heavy, held_as=jnp.bfloat16):
    result = deviation * jax.random.normal(key, extent, jnp.float32)
    if pieces:
        result = result * block_scale(key, extent, pieces, -0.22, 0.18)
    return jnp.clip(spiked(result, jax.random.fold_in(key, 3), *heavy), -bound, bound).astype(held_as)


def setup_inputs(seed: int = 0) -> dict:
    key_of = jax.random.split(jax.random.key(seed), 11)
    return {
        "fwd_before": bell_draw(key_of[0], (NSHOT, NZ, NX, NY), 1.0, 6.0, ((0, 16), (2, 8), (3, 4)), jnp.float32),
        "fwd_now": bell_draw(key_of[1], (NSHOT, NZ, NX, NY), 1.0, 6.0, ((0, 16), (2, 8), (3, 4)), jnp.float32),
        "adj_after": bell_draw(key_of[2], (NSHOT, NZ, NX, NY), 1.0, 6.0, ((0, 16), (2, 8), (3, 4)), jnp.float32),
        "adj_now": noise_with(key_of[3], (NSHOT, NZ, NX, NY), 1.0, 8.0, ((0, 16), (2, 8), (3, 4)), (0, 1, 16, 2.0), jnp.float32),
        "speed": jnp.clip(1.5 + 3.0 * jax.random.uniform(key_of[4], (NZ, NX, NY), jnp.float32) ** block_scale(key_of[4], (NZ, NX, NY), ((1, 8), (2, 4)), -0.2, 0.2), 1.5, 4.5),
        "src_pos": draw_src_pos(jax.random.fold_in(key_of[10], 71), 0),
        "src_amp": bell_draw(key_of[6], (NSHOT, 2, NSRC), 3.0, 12.0, ((0, 16),), jnp.float32),
        "rec_pos": draw_rec_pos(jax.random.fold_in(key_of[10], 71), 0),
        "observed": bell_draw(key_of[8], (NSHOT, 2, NREC), 1.0, 6.0, ((0, 16),), jnp.float32),
        "rate": jnp.clip(jnp.exp(jax.random.uniform(key_of[9], (1,), jnp.float32, math.log(0.05), math.log(0.2))), 0.05, 0.2),
    }


STENCIL_WEIGHTS = (-205.0 / 72.0, 1.6, -0.2, 8.0 / 315.0, -1.0 / 560.0)
TIME_FACTOR = 0.009


def stencil(padded, depth, rows, cols):
    total = 3.0 * STENCIL_WEIGHTS[0] * padded[4:4 + depth, 4:4 + rows, 4:4 + cols]
    for reach in range(1, 5):
        near = padded[4 + reach:4 + reach + depth, 4:4 + rows, 4:4 + cols] + padded[4 - reach:4 - reach + depth, 4:4 + rows, 4:4 + cols]
        near = near + padded[4:4 + depth, 4 + reach:4 + reach + rows, 4:4 + cols] + padded[4:4 + depth, 4 - reach:4 - reach + rows, 4:4 + cols]
        near = near + padded[4:4 + depth, 4:4 + rows, 4 + reach:4 + reach + cols] + padded[4:4 + depth, 4:4 + rows, 4 - reach:4 - reach + cols]
        total = total + STENCIL_WEIGHTS[reach] * near
    return total


def laplace(field):
    depth, rows, cols = field.shape
    return stencil(jnp.pad(field, 4), depth, rows, cols)


def reference(fwd_before, fwd_now, adj_after, adj_now, speed, src_pos, src_amp, rec_pos, observed, rate):
    coef = TIME_FACTOR * speed * speed

    def one_group(carry, inputs):
        before, current, after, adjoint, spos, samp, rpos, data = inputs
        lap_one = laplace(current)
        middle = 2.0 * current - before + coef * lap_one
        middle = middle.at[spos[:, 0], spos[:, 1], spos[:, 2]].add(samp[0])
        lap_two = laplace(middle)
        final = 2.0 * middle - current + coef * lap_two
        final = final.at[spos[:, 0], spos[:, 1], spos[:, 2]].add(samp[1])
        miss_two = middle[rpos[:, 0], rpos[:, 1], rpos[:, 2]] - data[0]
        miss_three = final[rpos[:, 0], rpos[:, 1], rpos[:, 2]] - data[1]
        adj_middle = 2.0 * adjoint - after + laplace(coef * adjoint)
        adj_middle = adj_middle.at[rpos[:, 0], rpos[:, 1], rpos[:, 2]].add(miss_three)
        adj_final = 2.0 * adj_middle - adjoint + laplace(coef * adj_middle)
        adj_final = adj_final.at[rpos[:, 0], rpos[:, 1], rpos[:, 2]].add(miss_two)
        image = adj_middle * lap_one + adjoint * lap_two
        term = 2.0 * TIME_FACTOR * speed * image
        return carry + term, (middle, final, adj_middle, adj_final)

    start = jnp.zeros(speed.shape, jnp.float32)
    total, outputs = lax.scan(one_group, start, (fwd_before, fwd_now, adj_after, adj_now, src_pos, src_amp, rec_pos, observed))
    new_speed = speed - rate[0] * total
    return outputs[0], outputs[1], outputs[2], outputs[3], new_speed, total
```

```python
import functools

import jax
import jax.numpy as jnp
from jax import lax
from jax.experimental import pallas as pl
from jax.experimental.pallas import tpu as pltpu
from jax.sharding import PartitionSpec as P

WEIGHTS = (-205.0 / 72.0, 1.6, -0.2, 8.0 / 315.0, -1.0 / 560.0)
TIME_FACTOR = 0.009
MESH = pl.DeviceIdType.MESH
NZ, ROWS, COLS = 32, 24, 128
NREC, NSRC = 256, 8
TILES = ROWS // 8
UNROLL = 4

(F_L, F_R, F_PL, F_PR, C_L, C_R, C_PL, C_PR, M_L, M_R, M_PL, M_PR, D_L, D_R, D_PL, D_PR) = range(16)
SUM_A, SUM_B, SUM_C, SUM_D, ALL_D, ALL_C, ALL_B, ALL_A = range(16, 24)
N_SEMS = 24


def kernel(
    before_h, now_h, after_h, adj_h, speed_h, src_pos, src_amp, rec_pos, observed, rate,
    mid_o, last_o, adj_mid_o, adj_last_o, new_o, grad_o,
    fnow, fmid, cadj, cmid,
    before, after, adj, speed, lap1, last, amid, alast,
    s_one, s_two, count, obs_two, obs_three,
    pack, halo,
    term, ra, sa, rb, sb, rc, sc, rd, grad, new,
    in_sem, out_sem, send_sem, recv_sem,
):
    shot, px, py = lax.axis_index("shot"), lax.axis_index("px"), lax.axis_index("py")
    n_px, n_py = lax.axis_size("px"), lax.axis_size("py")
    core, z_lo = lax.rem(shot, 2), shot // 2
    bit0, bit1, bit2 = lax.rem(z_lo, 2), lax.rem(z_lo // 2, 2), z_lo // 4
    has_left, has_right = px > 0, px < n_px - 1
    has_prev, has_next = py > 0, py < n_py - 1
    left = (shot, lax.rem(px + n_px - 1, n_px), py)
    right = (shot, lax.rem(px + 1, n_px), py)
    prev = (shot, px, lax.rem(py + n_py - 1, n_py))
    after_py = (shot, px, lax.rem(py + 1, n_py))
    mate = (shot + 1 - 2 * core, px, py)
    near1 = (shot + 2 * (1 - 2 * bit0), px, py)
    near2 = (shot + 4 * (1 - 2 * bit1), px, py)
    near4 = (shot + 8 * (1 - 2 * bit2), px, py)

    inner = (slice(4, 4 + NZ), slice(8, 8 + ROWS), slice(None))
    load_now = pltpu.make_async_copy(now_h, fnow.at[inner], in_sem.at[0])
    load_adj = pltpu.make_async_copy(adj_h, adj, in_sem.at[1])
    load_speed = pltpu.make_async_copy(speed_h, speed, in_sem.at[2])
    load_before = pltpu.make_async_copy(before_h, before, in_sem.at[3])
    load_after = pltpu.make_async_copy(after_h, after, in_sem.at[4])
    for load in (load_now, load_adj, load_speed, load_before, load_after):
        load.start()

    barrier = pltpu.get_barrier_semaphore()
    partners = (left, right, prev, after_py, mate, near1, near2, near4)
    for device in partners:
        pl.semaphore_signal(barrier, inc=1, device_id=device, device_id_type=MESH)

    for field in (fnow, fmid, cadj, cmid):
        for plane in (0, 1, 2, 3, NZ + 4, NZ + 5, NZ + 6, NZ + 7):
            field[plane] = jnp.zeros((ROWS + 16, COLS), jnp.float32)

    @pl.when(px == 0)
    def _():
        def body(z, _):
            for field in (fnow, fmid, cadj, cmid):
                field[z + 4, 0:8, :] = jnp.zeros((8, COLS), jnp.float32)
            return 0
        lax.fori_loop(0, NZ, body, 0)

    @pl.when(px == n_px - 1)
    def _():
        def body(z, _):
            for field in (fnow, fmid, cadj, cmid):
                field[z + 4, 8 + ROWS:16 + ROWS, :] = jnp.zeros((8, COLS), jnp.float32)
            return 0
        lax.fori_loop(0, NZ, body, 0)

    @pl.when(py == 0)
    def _():
        for k in range(4):
            halo[2 * k] = jnp.zeros((ROWS, COLS), jnp.float32)

    @pl.when(py == n_py - 1)
    def _():
        for k in range(4):
            halo[2 * k + 1] = jnp.zeros((ROWS, COLS), jnp.float32)

    lane = lax.broadcasted_iota(jnp.int32, (8, COLS), 1)
    group = lane // 4

    def remote(src, dst, sem, device):
        return pltpu.make_async_remote_copy(
            src_ref=src, dst_ref=dst, send_sem=send_sem.at[sem], recv_sem=recv_sem.at[sem],
            device_id=device, device_id_type=MESH,
        )

    class Halo:
        def __init__(self, k, field):
            low, high = slice(8, 12), slice(4 + ROWS, 8 + ROWS)
            over, under = slice(8 + ROWS, 12 + ROWS), slice(4, 8)
            depth = slice(4, 4 + NZ)
            self.to_left = remote(field.at[depth, low, :], field.at[depth, over, :], 4 * k, left)
            self.to_right = remote(field.at[depth, high, :], field.at[depth, under, :], 4 * k + 1, right)
            self.to_prev = remote(pack.at[2 * k], halo.at[2 * k + 1], 4 * k + 2, prev)
            self.to_next = remote(pack.at[2 * k + 1], halo.at[2 * k], 4 * k + 3, after_py)

        def send_left(self):
            pl.when(has_left)(self.to_left.start)

        def send_right(self):
            pl.when(has_right)(self.to_right.start)

        def send_lanes(self):
            pl.when(has_prev)(self.to_prev.start)
            pl.when(has_next)(self.to_next.start)

        def wait_left(self):
            pl.when(has_left)(self.to_right.wait_recv)

        def wait_right(self):
            pl.when(has_right)(self.to_left.wait_recv)

        def wait_lanes(self):
            pl.when(has_next)(self.to_prev.wait_recv)
            pl.when(has_prev)(self.to_next.wait_recv)

        def finish(self):
            pl.when(has_left)(self.to_left.wait_send)
            pl.when(has_right)(self.to_right.wait_send)
            pl.when(has_prev)(self.to_prev.wait_send)
            pl.when(has_next)(self.to_next.wait_send)

    halo_now, halo_cadj, halo_mid, halo_cmid = (
        Halo(k, field) for k, field in enumerate((fnow, cadj, fmid, cmid))
    )

    def packed(z, value, carry):
        to_prev, to_next = carry
        moved = pltpu.roll(value, lax.rem(4 * z + 4, COLS), 1)
        return (
            jnp.where(group == lax.rem(z + 1, NZ), moved, to_prev),
            jnp.where(group == z, moved, to_next),
        )

    def laplace(field, k, z, tile):
        row = 8 + 8 * tile
        centre = field[z + 4, row:row + 8, :]
        from_prev = pltpu.roll(halo[2 * k, 8 * tile:8 * tile + 8, :], COLS - 4 - 4 * z, 1)
        from_next = pltpu.roll(halo[2 * k + 1, 8 * tile:8 * tile + 8, :], COLS - 4 - 4 * z, 1)
        total = (3.0 * WEIGHTS[0]) * centre
        for r in range(1, 5):
            near = field[z + 4 + r, row:row + 8, :] + field[z + 4 - r, row:row + 8, :]
            near = near + field[z + 4, row + r:row + r + 8, :] + field[z + 4, row - r:row - r + 8, :]
            near = near + pltpu.roll(jnp.where(lane >= COLS - r, from_prev, centre), r, 1)
            near = near + pltpu.roll(jnp.where(lane < r, from_next, centre), COLS - r, 1)
            total = total + WEIGHTS[r] * near
        return centre, total

    zero = jnp.zeros((8, COLS), jnp.float32)

    def over_depth(tile, k, step):
        def body(z, carry):
            value = step(z)
            return packed(z, value, carry) if k is not None else carry
        carry = lax.fori_loop(0, NZ, body, (zero, zero) if k is not None else 0, unroll=UNROLL)
        if k is not None:
            pack[2 * k, 8 * tile:8 * tile + 8, :] = carry[0]
            pack[2 * k + 1, 8 * tile:8 * tile + 8, :] = carry[1]

    load_now.wait()
    pl.semaphore_wait(barrier, len(partners))
    halo_now.send_left()
    halo_now.send_right()
    for tile in range(TILES):
        over_depth(tile, 0, lambda z: fnow[z + 4, 8 + 8 * tile:16 + 8 * tile, :])
    halo_now.send_lanes()

    load_adj.wait()
    load_speed.wait()

    def coef_at(z, rows):
        value = speed[z, rows, :]
        return TIME_FACTOR * value * value

    for tile in range(TILES):
        rows, ext = slice(8 * tile, 8 * tile + 8), slice(8 + 8 * tile, 16 + 8 * tile)

        def scale(z):
            value = coef_at(z, rows) * adj[z, rows, :]
            cadj[z + 4, ext, :] = value
            return value

        over_depth(tile, 1, scale)
    halo_cadj.send_left()
    halo_cadj.send_right()
    halo_cadj.send_lanes()

    first_start, second_start = px * ROWS, py * COLS
    place = lax.broadcasted_iota(jnp.int32, (8, COLS), 0) * COLS + lane
    keys, amps = [], []
    for j in range(NSRC):
        first, second = src_pos[j, 1] - first_start, src_pos[j, 2] - second_start
        owned = (first >= 0) & (first < ROWS) & (second >= 0) & (second < COLS)
        keys.append(jnp.where(owned, (src_pos[j, 0] * ROWS + first) * COLS + second, -1))
        amps.append((src_amp[0, j], src_amp[1, j]))
    for tile in range(TILES):
        rows = slice(8 * tile, 8 * tile + 8)

        def sources(z, _):
            here = place + (z * ROWS + 8 * tile) * COLS
            one, two = zero, zero
            for key, (amp_one, amp_two) in zip(keys, amps):
                hit = here == key
                one = one + jnp.where(hit, amp_one, 0.0)
                two = two + jnp.where(hit, amp_two, 0.0)
            s_one[z, rows, :] = one
            s_two[z, rows, :] = two
            return 0

        lax.fori_loop(0, NZ, sources, 0)

    first = rec_pos[:, 1:2] - first_start
    second = rec_pos[:, 2:3] - second_start
    inside = (first >= 0) & (first < ROWS)
    cell = jnp.where(inside, rec_pos[:, 0:1] * ROWS + first, -1).astype(jnp.float32)
    cell_row = jnp.transpose(jnp.broadcast_to(cell, (NREC, COLS)))[0:1, :]
    data = jnp.transpose(observed[...])
    column = lax.broadcasted_iota(jnp.int32, (NREC, COLS), 1) == second
    parts = [column.astype(jnp.float32).astype(jnp.bfloat16)]
    for k in range(2):
        rest = jnp.where(column, jnp.broadcast_to(data[:, k:k + 1], (NREC, COLS)), 0.0)
        for _ in range(3):
            part = rest.astype(jnp.bfloat16)
            rest = rest - part.astype(jnp.float32)
            parts.append(part)
    DEPTHS = 8

    def receivers(step, _):
        base = step * (DEPTHS * ROWS)
        index = lax.broadcasted_iota(jnp.int32, (DEPTHS * ROWS, NREC), 0) + base
        hot = (index.astype(jnp.float32) == cell_row).astype(jnp.float32).astype(jnp.bfloat16)
        sums = [jnp.dot(hot, part, preferred_element_type=jnp.float32) for part in parts]
        depths = pl.ds(step * DEPTHS, DEPTHS)
        count[depths] = sums[0].reshape(DEPTHS, ROWS, COLS)
        obs_two[depths] = (sums[1] + sums[2] + sums[3]).reshape(DEPTHS, ROWS, COLS)
        obs_three[depths] = (sums[4] + sums[5] + sums[6]).reshape(DEPTHS, ROWS, COLS)
        return 0

    lax.fori_loop(0, NZ // DEPTHS, receivers, 0)

    load_before.wait()
    halo_now.wait_lanes()

    def mid_tile(tile):
        rows, ext = slice(8 * tile, 8 * tile + 8), slice(8 + 8 * tile, 16 + 8 * tile)

        def step(z):
            centre, lap = laplace(fnow, 0, z, tile)
            lap1[z, rows, :] = lap
            value = 2.0 * centre - before[z, rows, :] + coef_at(z, rows) * lap + s_one[z, rows, :]
            fmid[z + 4, ext, :] = value
            return value

        over_depth(tile, 2, step)

    mid_tile(1)
    halo_now.wait_left()
    mid_tile(0)
    halo_mid.send_left()
    halo_now.wait_right()
    mid_tile(2)
    halo_mid.send_right()
    halo_mid.send_lanes()
    store_mid = pltpu.make_async_copy(fmid.at[inner], mid_o, out_sem.at[0])
    store_mid.start()

    load_after.wait()
    halo_cadj.wait_lanes()

    def base_tile(tile):
        rows = slice(8 * tile, 8 * tile + 8)

        def step(z):
            _, lap = laplace(cadj, 1, z, tile)
            amid[z, rows, :] = 2.0 * adj[z, rows, :] - after[z, rows, :] + lap - obs_three[z, rows, :]

        over_depth(tile, None, step)

    base_tile(1)
    halo_cadj.wait_left()
    base_tile(0)
    halo_cadj.wait_right()
    base_tile(2)

    halo_mid.wait_lanes()

    def last_tile(tile):
        rows, ext = slice(8 * tile, 8 * tile + 8), slice(8 + 8 * tile, 16 + 8 * tile)

        def step(z):
            centre, lap = laplace(fmid, 2, z, tile)
            velocity = speed[z, rows, :]
            coef = TIME_FACTOR * velocity * velocity
            value = 2.0 * centre - fnow[z + 4, ext, :] + coef * lap + s_two[z, rows, :]
            last[z, rows, :] = value
            adjoint = amid[z, rows, :] + count[z, rows, :] * value
            amid[z, rows, :] = adjoint
            image = adjoint * lap1[z, rows, :] + adj[z, rows, :] * lap
            owner = z // 2
            term[owner // 8, lax.rem(owner // 4, 2), lax.rem(owner // 2, 2), lax.rem(owner, 2), lax.rem(z, 2), rows, :] = (
                2.0 * TIME_FACTOR * velocity * image
            )
            scaled = coef * adjoint
            cmid[z + 4, ext, :] = scaled
            return scaled

        over_depth(tile, 3, step)

    last_tile(1)
    halo_mid.wait_left()
    last_tile(0)
    halo_cmid.send_left()
    halo_mid.wait_right()
    last_tile(2)
    sum_a = remote(term.at[:, :, :, 1 - core], ra, SUM_A, mate)
    sum_a.start()
    halo_cmid.send_right()
    halo_cmid.send_lanes()
    store_last = pltpu.make_async_copy(last, last_o, out_sem.at[1])
    store_last.start()
    store_amid = pltpu.make_async_copy(amid, adj_mid_o, out_sem.at[2])
    store_amid.start()

    sum_a.wait_recv()

    def add_a(step, _):
        i, j = step // 2, lax.rem(step, 2)
        for k in range(2):
            sa[i, j, k] = term[i, j, k, core] + ra[i, j, k]
        return 0

    lax.fori_loop(0, 4, add_a, 0)
    sum_b = remote(sa.at[:, :, 1 - bit0], rb, SUM_B, near1)
    sum_b.start()
    sum_b.wait_recv()
    for i in range(2):
        for j in range(2):
            sb[i, j] = sa[i, j, bit0] + rb[i, j]
    sum_c = remote(sb.at[:, 1 - bit1], rc, SUM_C, near2)
    sum_c.start()

    def adj_tile(tile):
        rows = slice(8 * tile, 8 * tile + 8)
        ext = slice(8 + 8 * tile, 16 + 8 * tile)

        def step(z):
            _, lap = laplace(cmid, 3, z, tile)
            alast[z, rows, :] = (
                2.0 * amid[z, rows, :] - adj[z, rows, :] + lap
                + (count[z, rows, :] * fmid[z + 4, ext, :] - obs_two[z, rows, :])
            )

        over_depth(tile, None, step)

    halo_cmid.wait_lanes()
    adj_tile(1)

    sum_c.wait_recv()
    for i in range(2):
        sc[i] = sb[i, bit1] + rc[i]
    sum_d = remote(sc.at[1 - bit2], rd, SUM_D, near4)
    sum_d.start()
    sum_d.wait_recv()
    total = sc[bit2] + rd[...]
    grad[...] = total
    new[bit2, bit1, bit0, core] = speed[pl.ds(2 * shot, 2)] - rate[0] * total
    store_grad = pltpu.make_async_copy(grad, grad_o, out_sem.at[3])
    store_grad.start()

    own = new.at[bit2, bit1, bit0, core]
    all_d = remote(own, own, ALL_D, near4)
    all_d.start()
    all_d.wait_recv()
    own = new.at[:, bit1, bit0, core]
    all_c = remote(own, own, ALL_C, near2)
    all_c.start()
    all_c.wait_recv()
    own = new.at[:, :, bit0, core]
    all_b = remote(own, own, ALL_B, near1)
    all_b.start()
    all_b.wait_recv()
    own = new.at[:, :, :, core]
    all_a = remote(own, own, ALL_A, mate)
    all_a.start()

    halo_cmid.wait_left()
    adj_tile(0)
    halo_cmid.wait_right()
    adj_tile(2)
    store_alast = pltpu.make_async_copy(alast, adj_last_o, out_sem.at[4])
    store_alast.start()

    all_a.wait_recv()
    store_new = pltpu.make_async_copy(new, new_o, out_sem.at[5])
    store_new.start()

    for field in (halo_now, halo_cadj, halo_mid, halo_cmid):
        field.finish()
    for copy in (sum_a, sum_b, sum_c, sum_d, all_d, all_c, all_b, all_a):
        copy.wait_send()
    for store in (store_mid, store_last, store_amid, store_grad, store_alast, store_new):
        store.wait()


def local(before, now, after, adj, speed, src_pos, src_amp, rec_pos, observed, rate):
    f32 = jnp.float32
    block = (NZ, ROWS, COLS)
    padded = (NZ + 8, ROWS + 16, COLS)
    slab = (2, ROWS, COLS)

    def vmem(*shape):
        return pltpu.VMEM(shape, f32)

    anywhere = pl.BlockSpec(memory_space=pl.ANY)
    in_vmem = pl.BlockSpec(memory_space=pltpu.VMEM)
    in_smem = pl.BlockSpec(memory_space=pltpu.SMEM)
    outs = pl.pallas_call(
        kernel,
        out_shape=[jax.ShapeDtypeStruct(block, f32)] * 4
        + [jax.ShapeDtypeStruct((2, 2, 2, 2) + slab, f32), jax.ShapeDtypeStruct(slab, f32)],
        in_specs=[anywhere] * 5 + [in_smem, in_smem, in_vmem, in_vmem, in_smem],
        out_specs=[anywhere] * 6,
        scratch_shapes=[vmem(*padded)] * 4
        + [vmem(*block)] * 8
        + [vmem(*block)] * 5
        + [vmem(8, ROWS, COLS)] * 2
        + [
            vmem(2, 2, 2, 2, *slab),
            vmem(2, 2, 2, *slab), vmem(2, 2, 2, *slab),
            vmem(2, 2, *slab), vmem(2, 2, *slab),
            vmem(2, *slab), vmem(2, *slab),
            vmem(*slab), vmem(*slab),
            vmem(2, 2, 2, 2, *slab),
        ]
        + [
            pltpu.SemaphoreType.DMA((5,)),
            pltpu.SemaphoreType.DMA((6,)),
            pltpu.SemaphoreType.DMA((N_SEMS,)),
            pltpu.SemaphoreType.DMA((N_SEMS,)),
        ],
        compiler_params=pltpu.CompilerParams(
            collective_id=0, has_side_effects=True, vmem_limit_bytes=48 * 1024 * 1024
        ),
        name="window",
    )(
        before[0], now[0], after[0], adj[0], speed,
        src_pos[0], src_amp[0], rec_pos[0], observed[0], rate,
    )
    mid, last, adj_mid, adj_last, new, grad = outs
    return mid[None], last[None], adj_mid[None], adj_last[None], new.reshape(block), grad


def solution(mesh):
    wave = P("shot", None, "px", "py")
    group = P("shot", None, None)
    return jax.shard_map(
        local,
        mesh=mesh,
        in_specs=(wave, wave, wave, wave, P(None, "px", "py"), group, group, group, group, P()),
        out_specs=(wave, wave, wave, wave, P(None, "px", "py"), P("shot", "px", "py")),
        check_vma=False,
    )
```

```python
import functools

import jax
import jax.numpy as jnp
from jax import lax
from jax.experimental import pallas as pl
from jax.experimental.pallas import tpu as pltpu
from jax.sharding import PartitionSpec as P

WEIGHTS = (-205.0 / 72.0, 1.6, -0.2, 8.0 / 315.0, -1.0 / 560.0)
TIME_FACTOR = 0.009
MESH = pl.DeviceIdType.MESH
NZ, ROWS, COLS = 32, 24, 128
NREC, NSRC = 256, 8
TILES = ROWS // 8
UNROLL = 16

(F_L, F_R, F_PL, F_PR, C_L, C_R, C_PL, C_PR, M_L, M_R, M_PL, M_PR, D_L, D_R, D_PL, D_PR) = range(16)
SUM_A, SUM_B, SUM_C, SUM_D, ALL_D, ALL_C, ALL_B, ALL_A = range(16, 24)
N_SEMS = 24


def kernel(
    before_h, now_h, after_h, adj_h, speed_h, src_pos_h, src_amp_h, rec_pos_h, observed_h, rate,
    mid, last, amid, alast, new, grad,
    fnow, fmid, cadj, cmid,
    before, after, adj, speed, lap1,
    src_pos, src_amp, rec_pos, observed,
    s_one, s_two, count, obs_two, obs_three,
    pack, halo,
    term, ra, sa, rb, sb, rc, sc, rd,
    in_sem, send_sem, recv_sem,
):
    shot, px, py = lax.axis_index("shot"), lax.axis_index("px"), lax.axis_index("py")
    n_px, n_py = lax.axis_size("px"), lax.axis_size("py")
    core, z_lo = lax.rem(shot, 2), shot // 2
    bit0, bit1, bit2 = lax.rem(z_lo, 2), lax.rem(z_lo // 2, 2), z_lo // 4
    has_left, has_right = px > 0, px < n_px - 1
    has_prev, has_next = py > 0, py < n_py - 1
    left = (shot, lax.rem(px + n_px - 1, n_px), py)
    right = (shot, lax.rem(px + 1, n_px), py)
    prev = (shot, px, lax.rem(py + n_py - 1, n_py))
    after_py = (shot, px, lax.rem(py + 1, n_py))
    mate = (shot + 1 - 2 * core, px, py)
    near1 = (shot + 2 * (1 - 2 * bit0), px, py)
    near2 = (shot + 4 * (1 - 2 * bit1), px, py)
    near4 = (shot + 8 * (1 - 2 * bit2), px, py)

    inner = (slice(4, 4 + NZ), slice(8, 8 + ROWS), slice(None))
    load_now = pltpu.make_async_copy(now_h, fnow.at[inner], in_sem.at[0])
    load_adj = pltpu.make_async_copy(adj_h, adj, in_sem.at[1])
    load_speed = pltpu.make_async_copy(speed_h, speed, in_sem.at[2])
    load_before = pltpu.make_async_copy(before_h, before, in_sem.at[3])
    load_after = pltpu.make_async_copy(after_h, after, in_sem.at[4])
    load_small = [
        pltpu.make_async_copy(source, target, in_sem.at[5 + k])
        for k, (source, target) in enumerate(
            ((src_pos_h, src_pos), (src_amp_h, src_amp), (rec_pos_h, rec_pos), (observed_h, observed))
        )
    ]
    for load in (load_now, load_adj, load_speed, *load_small, load_before, load_after):
        load.start()

    barrier = pltpu.get_barrier_semaphore()
    partners = (left, right, prev, after_py, mate, near1, near2, near4)
    for device in partners:
        pl.semaphore_signal(barrier, inc=1, device_id=device, device_id_type=MESH)

    for field in (fnow, fmid, cadj, cmid):
        for plane in (0, 1, 2, 3, NZ + 4, NZ + 5, NZ + 6, NZ + 7):
            field[plane] = jnp.zeros((ROWS + 16, COLS), jnp.float32)

    @pl.when(px == 0)
    def _():
        def body(z, _):
            for field in (fnow, fmid, cadj, cmid):
                field[z + 4, 0:8, :] = jnp.zeros((8, COLS), jnp.float32)
            return 0
        lax.fori_loop(0, NZ, body, 0)

    @pl.when(px == n_px - 1)
    def _():
        def body(z, _):
            for field in (fnow, fmid, cadj, cmid):
                field[z + 4, 8 + ROWS:16 + ROWS, :] = jnp.zeros((8, COLS), jnp.float32)
            return 0
        lax.fori_loop(0, NZ, body, 0)

    @pl.when(py == 0)
    def _():
        for k in range(4):
            halo[2 * k] = jnp.zeros((ROWS, COLS), jnp.float32)

    @pl.when(py == n_py - 1)
    def _():
        for k in range(4):
            halo[2 * k + 1] = jnp.zeros((ROWS, COLS), jnp.float32)

    lane = lax.broadcasted_iota(jnp.int32, (8, COLS), 1)
    group = lane // 4

    def remote(src, dst, sem, device):
        return pltpu.make_async_remote_copy(
            src_ref=src, dst_ref=dst, send_sem=send_sem.at[sem], recv_sem=recv_sem.at[sem],
            device_id=device, device_id_type=MESH,
        )

    class Halo:
        def __init__(self, k, field):
            low, high = slice(8, 12), slice(4 + ROWS, 8 + ROWS)
            over, under = slice(8 + ROWS, 12 + ROWS), slice(4, 8)
            depth = slice(4, 4 + NZ)
            self.to_left = remote(field.at[depth, low, :], field.at[depth, over, :], 4 * k, left)
            self.to_right = remote(field.at[depth, high, :], field.at[depth, under, :], 4 * k + 1, right)
            self.to_prev = remote(pack.at[2 * k], halo.at[2 * k + 1], 4 * k + 2, prev)
            self.to_next = remote(pack.at[2 * k + 1], halo.at[2 * k], 4 * k + 3, after_py)

        def send_left(self):
            pl.when(has_left)(self.to_left.start)

        def send_right(self):
            pl.when(has_right)(self.to_right.start)

        def send_lanes(self):
            pl.when(has_prev)(self.to_prev.start)
            pl.when(has_next)(self.to_next.start)

        def wait_left(self):
            pl.when(has_left)(self.to_right.wait_recv)

        def wait_right(self):
            pl.when(has_right)(self.to_left.wait_recv)

        def wait_lanes(self):
            pl.when(has_next)(self.to_prev.wait_recv)
            pl.when(has_prev)(self.to_next.wait_recv)

        def finish(self):
            pl.when(has_left)(self.to_left.wait_send)
            pl.when(has_right)(self.to_right.wait_send)
            pl.when(has_prev)(self.to_prev.wait_send)
            pl.when(has_next)(self.to_next.wait_send)

    halo_now, halo_cadj, halo_mid, halo_cmid = (
        Halo(k, field) for k, field in enumerate((fnow, cadj, fmid, cmid))
    )

    def packed(z, value, carry):
        to_prev, to_next = carry
        moved = pltpu.roll(value, lax.rem(4 * z + 4, COLS), 1)
        return (
            jnp.where(group == lax.rem(z + 1, NZ), moved, to_prev),
            jnp.where(group == z, moved, to_next),
        )

    def laplace(field, k, z, tile):
        row = 8 + 8 * tile
        centre = field[z + 4, row:row + 8, :]
        from_prev = pltpu.roll(halo[2 * k, 8 * tile:8 * tile + 8, :], COLS - 4 - 4 * z, 1)
        from_next = pltpu.roll(halo[2 * k + 1, 8 * tile:8 * tile + 8, :], COLS - 4 - 4 * z, 1)
        total = (3.0 * WEIGHTS[0]) * centre
        for r in range(1, 5):
            near = field[z + 4 + r, row:row + 8, :] + field[z + 4 - r, row:row + 8, :]
            near = near + field[z + 4, row + r:row + r + 8, :] + field[z + 4, row - r:row - r + 8, :]
            near = near + pltpu.roll(jnp.where(lane >= COLS - r, from_prev, centre), r, 1)
            near = near + pltpu.roll(jnp.where(lane < r, from_next, centre), COLS - r, 1)
            total = total + WEIGHTS[r] * near
        return centre, total

    zero = jnp.zeros((8, COLS), jnp.float32)

    def over_depth(tile, k, step):
        def body(z, carry):
            value = step(z)
            return packed(z, value, carry) if k is not None else carry
        carry = lax.fori_loop(0, NZ, body, (zero, zero) if k is not None else 0, unroll=UNROLL)
        if k is not None:
            pack[2 * k, 8 * tile:8 * tile + 8, :] = carry[0]
            pack[2 * k + 1, 8 * tile:8 * tile + 8, :] = carry[1]

    load_now.wait()
    pl.semaphore_wait(barrier, len(partners))
    halo_now.send_left()
    halo_now.send_right()
    for tile in range(TILES):
        over_depth(tile, 0, lambda z: fnow[z + 4, 8 + 8 * tile:16 + 8 * tile, :])
    halo_now.send_lanes()

    load_adj.wait()
    load_speed.wait()

    def coef_at(z, rows):
        value = speed[z, rows, :]
        return TIME_FACTOR * value * value

    for tile in range(TILES):
        rows, ext = slice(8 * tile, 8 * tile + 8), slice(8 + 8 * tile, 16 + 8 * tile)

        def scale(z):
            value = coef_at(z, rows) * adj[z, rows, :]
            cadj[z + 4, ext, :] = value
            return value

        over_depth(tile, 1, scale)
    halo_cadj.send_left()
    halo_cadj.send_right()
    halo_cadj.send_lanes()

    for load in load_small:
        load.wait()
    first_start, second_start = px * ROWS, py * COLS
    place = lax.broadcasted_iota(jnp.int32, (8, COLS), 0) * COLS + lane
    first, second = src_pos[1] - first_start, src_pos[2] - second_start
    owned = (first >= 0) & (first < ROWS) & (second >= 0) & (second < COLS)
    key = jnp.where(owned, (src_pos[0] * ROWS + first) * COLS + second, -1)

    def spread(row, j):
        return jnp.broadcast_to(row[:, j:j + 1], (8, COLS))

    spikes = [(spread(key, j), spread(src_amp[0:1, :], j), spread(src_amp[1:2, :], j)) for j in range(NSRC)]
    for tile in range(TILES):
        rows = slice(8 * tile, 8 * tile + 8)

        def sources(z, _):
            here = place + (z * ROWS + 8 * tile) * COLS
            one, two = zero, zero
            for cell, amp_one, amp_two in spikes:
                hit = here == cell
                one = one + jnp.where(hit, amp_one, 0.0)
                two = two + jnp.where(hit, amp_two, 0.0)
            s_one[z, rows, :] = one
            s_two[z, rows, :] = two
            return 0

        lax.fori_loop(0, NZ, sources, 0, unroll=4)

    first = rec_pos[1] - first_start
    inside = (first >= 0) & (first < ROWS)
    cell_row = jnp.where(inside, rec_pos[0] * ROWS + first, -1).astype(jnp.float32)
    second = (rec_pos[2] - second_start).astype(jnp.float32)
    data = jnp.transpose(jnp.concatenate([second, observed[...], jnp.zeros((5, NREC), jnp.float32)], axis=0))
    column = lax.broadcasted_iota(jnp.int32, (NREC, COLS), 1).astype(jnp.float32) == data[:, 0:1]
    parts = [column.astype(jnp.float32).astype(jnp.bfloat16)]
    for k in range(2):
        rest = jnp.where(column, jnp.broadcast_to(data[:, k + 1:k + 2], (NREC, COLS)), 0.0)
        for _ in range(3):
            part = rest.astype(jnp.bfloat16)
            rest = rest - part.astype(jnp.float32)
            parts.append(part)
    DEPTHS = 8

    def receivers(step, _):
        base = step * (DEPTHS * ROWS)
        index = lax.broadcasted_iota(jnp.int32, (DEPTHS * ROWS, NREC), 0) + base
        hot = (index.astype(jnp.float32) == cell_row).astype(jnp.float32).astype(jnp.bfloat16)
        sums = [jnp.dot(hot, part, preferred_element_type=jnp.float32) for part in parts]
        depths = pl.ds(step * DEPTHS, DEPTHS)
        count[depths] = sums[0].reshape(DEPTHS, ROWS, COLS)
        obs_two[depths] = (sums[1] + sums[2] + sums[3]).reshape(DEPTHS, ROWS, COLS)
        obs_three[depths] = (sums[4] + sums[5] + sums[6]).reshape(DEPTHS, ROWS, COLS)
        return 0

    lax.fori_loop(0, NZ // DEPTHS, receivers, 0)

    load_before.wait()
    halo_now.wait_lanes()

    def mid_tile(tile):
        rows, ext = slice(8 * tile, 8 * tile + 8), slice(8 + 8 * tile, 16 + 8 * tile)

        def step(z):
            centre, lap = laplace(fnow, 0, z, tile)
            lap1[z, rows, :] = lap
            value = 2.0 * centre - before[z, rows, :] + coef_at(z, rows) * lap + s_one[z, rows, :]
            fmid[z + 4, ext, :] = value
            mid[z, rows, :] = value
            return value

        over_depth(tile, 2, step)

    mid_tile(1)
    halo_now.wait_left()
    mid_tile(0)
    halo_mid.send_left()
    halo_now.wait_right()
    mid_tile(2)
    halo_mid.send_right()
    halo_mid.send_lanes()

    load_after.wait()
    halo_cadj.wait_lanes()

    def base_tile(tile):
        rows = slice(8 * tile, 8 * tile + 8)

        def step(z):
            _, lap = laplace(cadj, 1, z, tile)
            amid[z, rows, :] = 2.0 * adj[z, rows, :] - after[z, rows, :] + lap - obs_three[z, rows, :]

        over_depth(tile, None, step)

    base_tile(1)
    halo_cadj.wait_left()
    base_tile(0)
    halo_cadj.wait_right()
    base_tile(2)

    halo_mid.wait_lanes()

    def last_tile(tile):
        rows, ext = slice(8 * tile, 8 * tile + 8), slice(8 + 8 * tile, 16 + 8 * tile)

        def step(z):
            centre, lap = laplace(fmid, 2, z, tile)
            velocity = speed[z, rows, :]
            coef = TIME_FACTOR * velocity * velocity
            value = 2.0 * centre - fnow[z + 4, ext, :] + coef * lap + s_two[z, rows, :]
            last[z, rows, :] = value
            adjoint = amid[z, rows, :] + count[z, rows, :] * value
            amid[z, rows, :] = adjoint
            image = adjoint * lap1[z, rows, :] + adj[z, rows, :] * lap
            owner = z // 2
            term[owner // 8, lax.rem(owner // 4, 2), lax.rem(owner // 2, 2), lax.rem(owner, 2), lax.rem(z, 2), rows, :] = (
                2.0 * TIME_FACTOR * velocity * image
            )
            scaled = coef * adjoint
            cmid[z + 4, ext, :] = scaled
            return scaled

        over_depth(tile, 3, step)

    last_tile(1)
    halo_mid.wait_left()
    last_tile(0)
    halo_cmid.send_left()
    halo_mid.wait_right()
    last_tile(2)
    sum_a = remote(term.at[:, :, :, 1 - core], ra, SUM_A, mate)
    sum_a.start()
    halo_cmid.send_right()
    halo_cmid.send_lanes()

    sum_a.wait_recv()

    def add_a(step, _):
        i, j = step // 2, lax.rem(step, 2)
        for k in range(2):
            sa[i, j, k] = term[i, j, k, core] + ra[i, j, k]
        return 0

    lax.fori_loop(0, 4, add_a, 0)
    sum_b = remote(sa.at[:, :, 1 - bit0], rb, SUM_B, near1)
    sum_b.start()
    sum_b.wait_recv()
    for i in range(2):
        for j in range(2):
            sb[i, j] = sa[i, j, bit0] + rb[i, j]
    sum_c = remote(sb.at[:, 1 - bit1], rc, SUM_C, near2)
    sum_c.start()

    def adj_tile(tile):
        rows = slice(8 * tile, 8 * tile + 8)
        ext = slice(8 + 8 * tile, 16 + 8 * tile)

        def step(z):
            _, lap = laplace(cmid, 3, z, tile)
            alast[z, rows, :] = (
                2.0 * amid[z, rows, :] - adj[z, rows, :] + lap
                + (count[z, rows, :] * fmid[z + 4, ext, :] - obs_two[z, rows, :])
            )

        over_depth(tile, None, step)

    halo_cmid.wait_lanes()
    adj_tile(1)

    sum_c.wait_recv()
    for i in range(2):
        sc[i] = sb[i, bit1] + rc[i]
    sum_d = remote(sc.at[1 - bit2], rd, SUM_D, near4)
    sum_d.start()
    sum_d.wait_recv()
    total = sc[bit2] + rd[...]
    grad[...] = total
    new[bit2, bit1, bit0, core] = speed[pl.ds(2 * shot, 2)] - rate[0] * total

    own = new.at[bit2, bit1, bit0, core]
    all_d = remote(own, own, ALL_D, near4)
    all_d.start()
    all_d.wait_recv()
    own = new.at[:, bit1, bit0, core]
    all_c = remote(own, own, ALL_C, near2)
    all_c.start()
    all_c.wait_recv()
    own = new.at[:, :, bit0, core]
    all_b = remote(own, own, ALL_B, near1)
    all_b.start()
    all_b.wait_recv()
    own = new.at[:, :, :, core]
    all_a = remote(own, own, ALL_A, mate)
    all_a.start()

    halo_cmid.wait_left()
    adj_tile(0)
    halo_cmid.wait_right()
    adj_tile(2)

    all_a.wait_recv()

    for field in (halo_now, halo_cadj, halo_mid, halo_cmid):
        field.finish()
    for copy in (sum_a, sum_b, sum_c, sum_d, all_d, all_c, all_b, all_a):
        copy.wait_send()


def write(*refs):
    sem = refs[12]
    copies = [pltpu.make_async_copy(refs[k], refs[6 + k], sem.at[k]) for k in range(6)]
    for copy in copies:
        copy.start()
    for copy in copies:
        copy.wait()


def local(before, now, after, adj, speed, src_pos, src_amp, rec_pos, observed, rate):
    f32 = jnp.float32
    block = (NZ, ROWS, COLS)
    padded = (NZ + 8, ROWS + 16, COLS)
    slab = (2, ROWS, COLS)

    def vmem(*shape):
        return pltpu.VMEM(shape, f32)

    in_hbm = pl.BlockSpec(memory_space=pltpu.HBM)
    in_vmem = pl.BlockSpec(memory_space=pltpu.VMEM)
    in_smem = pl.BlockSpec(memory_space=pltpu.SMEM)
    outs = pl.pallas_call(
        kernel,
        out_shape=[jax.ShapeDtypeStruct(block, f32)] * 4
        + [jax.ShapeDtypeStruct((2, 2, 2, 2) + slab, f32), jax.ShapeDtypeStruct(slab, f32)],
        in_specs=[in_hbm] * 9 + [in_smem],
        out_specs=[in_vmem] * 6,
        scratch_shapes=[vmem(*padded)] * 4
        + [vmem(*block)] * 5
        + [
            pltpu.VMEM((3, 1, NSRC), jnp.int32), vmem(2, NSRC),
            pltpu.VMEM((3, 1, NREC), jnp.int32), vmem(2, NREC),
        ]
        + [vmem(*block)] * 5
        + [vmem(8, ROWS, COLS)] * 2
        + [
            vmem(2, 2, 2, 2, *slab),
            vmem(2, 2, 2, *slab), vmem(2, 2, 2, *slab),
            vmem(2, 2, *slab), vmem(2, 2, *slab),
            vmem(2, *slab), vmem(2, *slab),
            vmem(*slab),
        ]
        + [
            pltpu.SemaphoreType.DMA((9,)),
            pltpu.SemaphoreType.DMA((N_SEMS,)),
            pltpu.SemaphoreType.DMA((N_SEMS,)),
        ],
        compiler_params=pltpu.CompilerParams(
            collective_id=0, has_side_effects=True, vmem_limit_bytes=53100 * 1024
        ),
        name="window",
    )(
        before[0], now[0], after[0], adj[0], speed,
        src_pos.transpose(2, 0, 1), src_amp[0], rec_pos.transpose(2, 0, 1), observed[0], rate,
    )
    mid, last, adj_mid, adj_last, new, grad = pl.pallas_call(
        write,
        out_shape=[jax.ShapeDtypeStruct(out.shape, f32) for out in outs],
        in_specs=[in_vmem] * 6,
        out_specs=[in_hbm] * 6,
        scratch_shapes=[pltpu.SemaphoreType.DMA((6,))],
        compiler_params=pltpu.CompilerParams(vmem_limit_bytes=1024 * 1024),
        name="write",
    )(*outs)
    return mid[None], last[None], adj_mid[None], adj_last[None], new.reshape(block), grad


def solution(mesh):
    wave = P("shot", None, "px", "py")
    group = P("shot", None, None)
    return jax.shard_map(
        local,
        mesh=mesh,
        in_specs=(wave, wave, wave, wave, P(None, "px", "py"), group, group, group, group, P()),
        out_specs=(wave, wave, wave, wave, P(None, "px", "py"), P("shot", "px", "py")),
        check_vma=False,
    )
```

```python
import functools

import jax
import jax.numpy as jnp
from jax import lax
from jax.experimental import pallas as pl
from jax.experimental.pallas import tpu as pltpu
from jax.sharding import PartitionSpec as P

WEIGHTS = (-205.0 / 72.0, 1.6, -0.2, 8.0 / 315.0, -1.0 / 560.0)
TIME_FACTOR = 0.009
MESH = pl.DeviceIdType.MESH
NZ, ROWS, COLS = 32, 24, 128
NREC, NSRC = 256, 8
TILES = ROWS // 8
UNROLL = 16

(F_L, F_R, F_PL, F_PR, C_L, C_R, C_PL, C_PR, M_L, M_R, M_PL, M_PR, D_L, D_R, D_PL, D_PR) = range(16)
SUM_A, SUM_D, ALL_A = range(16, 19)
SUM_B, ALL_B = 18, 21
N_SEMS = 25


def kernel(
    before_h, now_h, after_h, adj_h, speed_h, src_pos_h, src_amp_h, rec_pos_h, observed_h, rate,
    mid, last, amid, alast, new, grad,
    fnow, fmid, cadj, cmid,
    before, after, adj, speed, lap1,
    src_pos, src_amp, rec_pos, observed,
    s_one, s_two, count, obs_two, obs_three,
    pack, halo,
    term, ra, sa, rb, sc, rd,
    in_sem, send_sem, recv_sem,
):
    shot, px, py = lax.axis_index("shot"), lax.axis_index("px"), lax.axis_index("py")
    n_px, n_py = lax.axis_size("px"), lax.axis_size("py")
    core, z_lo = lax.rem(shot, 2), shot // 2
    bit0, bit1, bit2 = lax.rem(z_lo, 2), lax.rem(z_lo // 2, 2), z_lo // 4
    has_left, has_right = px > 0, px < n_px - 1
    has_prev, has_next = py > 0, py < n_py - 1
    left = (shot, lax.rem(px + n_px - 1, n_px), py)
    right = (shot, lax.rem(px + 1, n_px), py)
    prev = (shot, px, lax.rem(py + n_py - 1, n_py))
    after_py = (shot, px, lax.rem(py + 1, n_py))
    mate = (shot + 1 - 2 * core, px, py)
    near1 = (shot + 2 * (1 - 2 * bit0), px, py)
    near2 = (shot + 4 * (1 - 2 * bit1), px, py)
    near3 = (shot + 2 * (1 - 2 * bit0) + 4 * (1 - 2 * bit1), px, py)
    near4 = (shot + 8 * (1 - 2 * bit2), px, py)

    inner = (slice(4, 4 + NZ), slice(8, 8 + ROWS), slice(None))
    load_now = pltpu.make_async_copy(now_h, fnow.at[inner], in_sem.at[0])
    load_adj = pltpu.make_async_copy(adj_h, adj, in_sem.at[1])
    load_speed = pltpu.make_async_copy(speed_h, speed, in_sem.at[2])
    load_before = pltpu.make_async_copy(before_h, before, in_sem.at[3])
    load_after = pltpu.make_async_copy(after_h, after, in_sem.at[4])
    load_small = [
        pltpu.make_async_copy(source, target, in_sem.at[5 + k])
        for k, (source, target) in enumerate(
            ((src_pos_h, src_pos), (src_amp_h, src_amp), (rec_pos_h, rec_pos), (observed_h, observed))
        )
    ]
    for load in (load_now, load_adj, load_speed, *load_small, load_before, load_after):
        load.start()

    barrier = pltpu.get_barrier_semaphore()
    partners = (left, right, prev, after_py, mate, near1, near2, near3, near4)
    for device in partners:
        pl.semaphore_signal(barrier, inc=1, device_id=device, device_id_type=MESH)

    for field in (fnow, fmid, cadj, cmid):
        for plane in (0, 1, 2, 3, NZ + 4, NZ + 5, NZ + 6, NZ + 7):
            field[plane] = jnp.zeros((ROWS + 16, COLS), jnp.float32)

    @pl.when(px == 0)
    def _():
        def body(z, _):
            for field in (fnow, fmid, cadj, cmid):
                field[z + 4, 0:8, :] = jnp.zeros((8, COLS), jnp.float32)
            return 0
        lax.fori_loop(0, NZ, body, 0)

    @pl.when(px == n_px - 1)
    def _():
        def body(z, _):
            for field in (fnow, fmid, cadj, cmid):
                field[z + 4, 8 + ROWS:16 + ROWS, :] = jnp.zeros((8, COLS), jnp.float32)
            return 0
        lax.fori_loop(0, NZ, body, 0)

    @pl.when(py == 0)
    def _():
        for k in range(4):
            halo[2 * k] = jnp.zeros((ROWS, COLS), jnp.float32)

    @pl.when(py == n_py - 1)
    def _():
        for k in range(4):
            halo[2 * k + 1] = jnp.zeros((ROWS, COLS), jnp.float32)

    lane = lax.broadcasted_iota(jnp.int32, (8, COLS), 1)
    group = lane // 4

    def remote(src, dst, sem, device):
        return pltpu.make_async_remote_copy(
            src_ref=src, dst_ref=dst, send_sem=send_sem.at[sem], recv_sem=recv_sem.at[sem],
            device_id=device, device_id_type=MESH,
        )

    class Halo:
        def __init__(self, k, field):
            low, high = slice(8, 12), slice(4 + ROWS, 8 + ROWS)
            over, under = slice(8 + ROWS, 12 + ROWS), slice(4, 8)
            depth = slice(4, 4 + NZ)
            self.to_left = remote(field.at[depth, low, :], field.at[depth, over, :], 4 * k, left)
            self.to_right = remote(field.at[depth, high, :], field.at[depth, under, :], 4 * k + 1, right)
            self.to_prev = remote(pack.at[2 * k], halo.at[2 * k + 1], 4 * k + 2, prev)
            self.to_next = remote(pack.at[2 * k + 1], halo.at[2 * k], 4 * k + 3, after_py)

        def send_left(self):
            pl.when(has_left)(self.to_left.start)

        def send_right(self):
            pl.when(has_right)(self.to_right.start)

        def send_lanes(self):
            pl.when(has_prev)(self.to_prev.start)
            pl.when(has_next)(self.to_next.start)

        def wait_left(self):
            pl.when(has_left)(self.to_right.wait_recv)

        def wait_right(self):
            pl.when(has_right)(self.to_left.wait_recv)

        def wait_lanes(self):
            pl.when(has_next)(self.to_prev.wait_recv)
            pl.when(has_prev)(self.to_next.wait_recv)

        drained = False

        def drain(self):
            if not self.drained:
                pl.when(has_left)(self.to_left.wait_send)
                pl.when(has_right)(self.to_right.wait_send)
            self.drained = True

        def finish(self):
            self.drain()
            pl.when(has_prev)(self.to_prev.wait_send)
            pl.when(has_next)(self.to_next.wait_send)

    halo_now, halo_cadj, halo_mid, halo_cmid = (
        Halo(k, field) for k, field in enumerate((fnow, cadj, fmid, cmid))
    )

    def packed(z, value, carry):
        to_prev, to_next = carry
        moved = pltpu.roll(value, lax.rem(4 * z + 4, COLS), 1)
        return (
            jnp.where(group == lax.rem(z + 1, NZ), moved, to_prev),
            jnp.where(group == z, moved, to_next),
        )

    def laplace(field, k, z, tile):
        row = 8 + 8 * tile
        centre = field[z + 4, row:row + 8, :]
        from_prev = pltpu.roll(halo[2 * k, 8 * tile:8 * tile + 8, :], COLS - 4 - 4 * z, 1)
        from_next = pltpu.roll(halo[2 * k + 1, 8 * tile:8 * tile + 8, :], COLS - 4 - 4 * z, 1)
        total = (3.0 * WEIGHTS[0]) * centre
        for r in range(1, 5):
            near = field[z + 4 + r, row:row + 8, :] + field[z + 4 - r, row:row + 8, :]
            near = near + field[z + 4, row + r:row + r + 8, :] + field[z + 4, row - r:row - r + 8, :]
            near = near + pltpu.roll(jnp.where(lane >= COLS - r, from_prev, centre), r, 1)
            near = near + pltpu.roll(jnp.where(lane < r, from_next, centre), COLS - r, 1)
            total = total + WEIGHTS[r] * near
        return centre, total

    zero = jnp.zeros((8, COLS), jnp.float32)

    def over_depth(tile, k, step):
        def body(z, carry):
            value = step(z)
            return packed(z, value, carry) if k is not None else carry
        carry = lax.fori_loop(0, NZ, body, (zero, zero) if k is not None else 0, unroll=UNROLL)
        if k is not None:
            pack[2 * k, 8 * tile:8 * tile + 8, :] = carry[0]
            pack[2 * k + 1, 8 * tile:8 * tile + 8, :] = carry[1]

    load_now.wait()
    pl.semaphore_wait(barrier, len(partners))
    halo_now.send_left()
    halo_now.send_right()
    for tile in range(TILES):
        over_depth(tile, 0, lambda z: fnow[z + 4, 8 + 8 * tile:16 + 8 * tile, :])
    halo_now.send_lanes()

    load_adj.wait()
    load_speed.wait()

    def coef_at(z, rows):
        value = speed[z, rows, :]
        return TIME_FACTOR * value * value

    for tile in range(TILES):
        rows, ext = slice(8 * tile, 8 * tile + 8), slice(8 + 8 * tile, 16 + 8 * tile)

        def scale(z):
            value = coef_at(z, rows) * adj[z, rows, :]
            cadj[z + 4, ext, :] = value
            return value

        over_depth(tile, 1, scale)
    halo_cadj.send_lanes()

    for load in load_small:
        load.wait()
    first_start, second_start = px * ROWS, py * COLS
    place = lax.broadcasted_iota(jnp.int32, (8, COLS), 0) * COLS + lane
    first, second = src_pos[1] - first_start, src_pos[2] - second_start
    owned = (first >= 0) & (first < ROWS) & (second >= 0) & (second < COLS)
    key = jnp.where(owned, (src_pos[0] * ROWS + first) * COLS + second, -1)

    def spread(row, j):
        return jnp.broadcast_to(row[:, j:j + 1], (8, COLS))

    spikes = [(spread(key, j), spread(src_amp[0:1, :], j), spread(src_amp[1:2, :], j)) for j in range(NSRC)]
    for tile in range(TILES):
        rows = slice(8 * tile, 8 * tile + 8)

        def sources(z, _):
            here = place + (z * ROWS + 8 * tile) * COLS
            one, two = zero, zero
            for cell, amp_one, amp_two in spikes:
                hit = here == cell
                one = one + jnp.where(hit, amp_one, 0.0)
                two = two + jnp.where(hit, amp_two, 0.0)
            s_one[z, rows, :] = one
            s_two[z, rows, :] = two
            return 0

        lax.fori_loop(0, NZ, sources, 0, unroll=4)

    first = rec_pos[1] - first_start
    inside = (first >= 0) & (first < ROWS)
    cell_row = jnp.where(inside, rec_pos[0] * ROWS + first, -1).astype(jnp.float32)
    second = (rec_pos[2] - second_start).astype(jnp.float32)
    data = jnp.transpose(jnp.concatenate([second, observed[...], jnp.zeros((5, NREC), jnp.float32)], axis=0))
    column = lax.broadcasted_iota(jnp.int32, (NREC, COLS), 1).astype(jnp.float32) == data[:, 0:1]
    parts = [column.astype(jnp.float32).astype(jnp.bfloat16)]
    for k in range(2):
        rest = jnp.where(column, jnp.broadcast_to(data[:, k + 1:k + 2], (NREC, COLS)), 0.0)
        for _ in range(3):
            part = rest.astype(jnp.bfloat16)
            rest = rest - part.astype(jnp.float32)
            parts.append(part)
    DEPTHS = 8

    def receivers(step, _):
        base = step * (DEPTHS * ROWS)
        index = lax.broadcasted_iota(jnp.int32, (DEPTHS * ROWS, NREC), 0) + base
        hot = (index.astype(jnp.float32) == cell_row).astype(jnp.float32).astype(jnp.bfloat16)
        sums = [jnp.dot(hot, part, preferred_element_type=jnp.float32) for part in parts]
        depths = pl.ds(step * DEPTHS, DEPTHS)
        count[depths] = sums[0].reshape(DEPTHS, ROWS, COLS)
        obs_two[depths] = (sums[1] + sums[2] + sums[3]).reshape(DEPTHS, ROWS, COLS)
        obs_three[depths] = (sums[4] + sums[5] + sums[6]).reshape(DEPTHS, ROWS, COLS)
        return 0

    lax.fori_loop(0, NZ // DEPTHS, receivers, 0)
    halo_now.drain()
    halo_cadj.send_left()
    halo_cadj.send_right()

    load_before.wait()
    halo_now.wait_lanes()

    def mid_tile(tile):
        rows, ext = slice(8 * tile, 8 * tile + 8), slice(8 + 8 * tile, 16 + 8 * tile)

        def step(z):
            centre, lap = laplace(fnow, 0, z, tile)
            lap1[z, rows, :] = lap
            value = 2.0 * centre - before[z, rows, :] + coef_at(z, rows) * lap + s_one[z, rows, :]
            fmid[z + 4, ext, :] = value
            mid[z, rows, :] = value
            return value

        over_depth(tile, 2, step)

    mid_tile(1)
    halo_now.wait_left()
    mid_tile(0)
    halo_mid.send_left()
    halo_now.wait_right()
    mid_tile(2)
    halo_mid.send_right()
    halo_mid.send_lanes()

    load_after.wait()
    halo_cadj.wait_lanes()

    def base_tile(tile):
        rows = slice(8 * tile, 8 * tile + 8)

        def step(z):
            _, lap = laplace(cadj, 1, z, tile)
            amid[z, rows, :] = 2.0 * adj[z, rows, :] - after[z, rows, :] + lap - obs_three[z, rows, :]

        over_depth(tile, None, step)

    base_tile(1)
    halo_cadj.wait_left()
    base_tile(0)
    halo_cadj.wait_right()
    base_tile(2)

    halo_mid.wait_lanes()

    def last_tile(tile):
        rows, ext = slice(8 * tile, 8 * tile + 8), slice(8 + 8 * tile, 16 + 8 * tile)

        def step(z):
            centre, lap = laplace(fmid, 2, z, tile)
            velocity = speed[z, rows, :]
            coef = TIME_FACTOR * velocity * velocity
            value = 2.0 * centre - fnow[z + 4, ext, :] + coef * lap + s_two[z, rows, :]
            last[z, rows, :] = value
            adjoint = amid[z, rows, :] + count[z, rows, :] * value
            amid[z, rows, :] = adjoint
            image = adjoint * lap1[z, rows, :] + adj[z, rows, :] * lap
            owner = z // 2
            term[owner // 8, lax.rem(owner // 4, 2), lax.rem(owner // 2, 2), lax.rem(owner, 2), lax.rem(z, 2), rows, :] = (
                2.0 * TIME_FACTOR * velocity * image
            )
            scaled = coef * adjoint
            cmid[z + 4, ext, :] = scaled
            return scaled

        over_depth(tile, 3, step)

    last_tile(1)
    halo_mid.wait_left()
    last_tile(0)
    halo_cmid.send_left()
    halo_mid.wait_right()
    last_tile(2)
    sum_a = remote(term.at[:, :, :, 1 - core], ra, SUM_A, mate)
    sum_a.start()
    halo_cmid.send_right()
    halo_cmid.send_lanes()

    sum_a.wait_recv()

    def add_a(step, _):
        i, j = step // 2, lax.rem(step, 2)
        for k in range(2):
            sa[i, j, k] = term[i, j, k, core] + ra[i, j, k]
        return 0

    lax.fori_loop(0, 4, add_a, 0)
    others = ((3, near3, 1 - bit1, 1 - bit0), (2, near2, 1 - bit1, bit0), (1, near1, bit1, 1 - bit0))
    sums = [remote(sa.at[:, i, j], rb.at[k - 1], SUM_B + k, device) for k, device, i, j in others]
    for copy in sums:
        copy.start()

    def adj_tile(tile):
        rows = slice(8 * tile, 8 * tile + 8)
        ext = slice(8 + 8 * tile, 16 + 8 * tile)

        def step(z):
            _, lap = laplace(cmid, 3, z, tile)
            alast[z, rows, :] = (
                2.0 * amid[z, rows, :] - adj[z, rows, :] + lap
                + (count[z, rows, :] * fmid[z + 4, ext, :] - obs_two[z, rows, :])
            )

        over_depth(tile, None, step)

    halo_cmid.wait_lanes()
    adj_tile(1)

    for copy in sums:
        copy.wait_recv()
    for i in range(2):
        sc[i] = sa[i, bit1, bit0] + rb[0, i] + rb[1, i] + rb[2, i]
    sum_d = remote(sc, rd, SUM_D, near4)
    sum_d.start()
    sum_d.wait_recv()
    for i in range(2):
        new[i, bit1, bit0, core] = speed[pl.ds(16 * i + 2 * lax.rem(shot, 8), 2)] - rate[0] * (sc[i] + rd[i])

    own = new.at[:, bit1, bit0, core]
    gathers = [remote(own, own, ALL_B + k, device) for k, device, _, _ in others]
    for copy in gathers:
        copy.start()
    grad[...] = sc[bit2] + rd[bit2]
    halo_cmid.wait_left()
    adj_tile(0)
    halo_cmid.wait_right()
    adj_tile(2)
    for copy in gathers:
        copy.wait_recv()
    own = new.at[:, :, :, core]
    all_a = remote(own, own, ALL_A, mate)
    all_a.start()


    all_a.wait_recv()

    for field in (halo_now, halo_cadj, halo_mid, halo_cmid):
        field.finish()
    for copy in (sum_a, *sums, sum_d, *gathers, all_a):
        copy.wait_send()


def write(*refs):
    sem = refs[12]
    copies = [pltpu.make_async_copy(refs[k], refs[6 + k], sem.at[k]) for k in range(6)]
    for copy in copies:
        copy.start()
    for copy in copies:
        copy.wait()


def local(before, now, after, adj, speed, src_pos, src_amp, rec_pos, observed, rate):
    f32 = jnp.float32
    block = (NZ, ROWS, COLS)
    padded = (NZ + 8, ROWS + 16, COLS)
    slab = (2, ROWS, COLS)

    def vmem(*shape):
        return pltpu.VMEM(shape, f32)

    in_hbm = pl.BlockSpec(memory_space=pltpu.HBM)
    in_vmem = pl.BlockSpec(memory_space=pltpu.VMEM)
    in_smem = pl.BlockSpec(memory_space=pltpu.SMEM)
    outs = pl.pallas_call(
        kernel,
        out_shape=[jax.ShapeDtypeStruct(block, f32)] * 4
        + [jax.ShapeDtypeStruct((2, 2, 2, 2) + slab, f32), jax.ShapeDtypeStruct(slab, f32)],
        in_specs=[in_hbm] * 9 + [in_smem],
        out_specs=[in_vmem] * 6,
        scratch_shapes=[vmem(*padded)] * 4
        + [vmem(*block)] * 5
        + [
            pltpu.VMEM((3, 1, NSRC), jnp.int32), vmem(2, NSRC),
            pltpu.VMEM((3, 1, NREC), jnp.int32), vmem(2, NREC),
        ]
        + [vmem(*block)] * 5
        + [vmem(8, ROWS, COLS)] * 2
        + [
            vmem(2, 2, 2, 2, *slab),
            vmem(2, 2, 2, *slab), vmem(2, 2, 2, *slab),
            vmem(3, 2, *slab),
            vmem(2, *slab), vmem(2, *slab),
        ]
        + [
            pltpu.SemaphoreType.DMA((9,)),
            pltpu.SemaphoreType.DMA((N_SEMS,)),
            pltpu.SemaphoreType.DMA((N_SEMS,)),
        ],
        compiler_params=pltpu.CompilerParams(
            collective_id=0, has_side_effects=True, vmem_limit_bytes=53100 * 1024
        ),
        name="window",
    )(
        before[0], now[0], after[0], adj[0], speed,
        src_pos.transpose(2, 0, 1), src_amp[0], rec_pos.transpose(2, 0, 1), observed[0], rate,
    )
    mid, last, adj_mid, adj_last, new, grad = pl.pallas_call(
        write,
        out_shape=[jax.ShapeDtypeStruct(out.shape, f32) for out in outs],
        in_specs=[in_vmem] * 6,
        out_specs=[in_hbm] * 6,
        scratch_shapes=[pltpu.SemaphoreType.DMA((6,))],
        compiler_params=pltpu.CompilerParams(vmem_limit_bytes=1024 * 1024),
        name="write",
    )(*outs)
    return mid[None], last[None], adj_mid[None], adj_last[None], new.reshape(block), grad


def solution(mesh):
    wave = P("shot", None, "px", "py")
    group = P("shot", None, None)
    return jax.shard_map(
        local,
        mesh=mesh,
        in_specs=(wave, wave, wave, wave, P(None, "px", "py"), group, group, group, group, P()),
        out_specs=(wave, wave, wave, wave, P(None, "px", "py"), P("shot", "px", "py")),
        check_vma=False,
    )
```

```python
import functools

import jax
import jax.numpy as jnp
from jax import lax
from jax.experimental import pallas as pl
from jax.experimental.pallas import tpu as pltpu
from jax.sharding import PartitionSpec as P

WEIGHTS = (-205.0 / 72.0, 1.6, -0.2, 8.0 / 315.0, -1.0 / 560.0)
TIME_FACTOR = 0.009
MESH = pl.DeviceIdType.MESH
NZ, ROWS, COLS = 32, 24, 128
NREC, NSRC = 256, 8
TILES = ROWS // 8
UNROLL = 16

(F_L, F_R, F_PL, F_PR, C_L, C_R, C_PL, C_PR, M_L, M_R, M_PL, M_PR, D_L, D_R, D_PL, D_PR) = range(16)
SUM_A, SUM_D, ALL_A = range(16, 19)
SUM_B, ALL_B = 18, 21
N_SEMS = 25


def kernel(
    before_h, now_h, after_h, adj_h, speed_h, src_pos_h, src_amp_h, rec_pos_h, observed_h, rate,
    mid, last, amid, alast, new, grad,
    fnow, fmid, cadj, cmid,
    before, after, adj, speed, lap1,
    src_pos, src_amp, rec_pos, observed,
    s_one, s_two, count, obs_two, obs_three,
    pack, halo,
    term, ra, sa, rb, sc, rd,
    in_sem, send_sem, recv_sem,
):
    shot, px, py = lax.axis_index("shot"), lax.axis_index("px"), lax.axis_index("py")
    n_px, n_py = lax.axis_size("px"), lax.axis_size("py")
    core, z_lo = lax.rem(shot, 2), shot // 2
    bit0, bit1, bit2 = lax.rem(z_lo, 2), lax.rem(z_lo // 2, 2), z_lo // 4
    has_left, has_right = px > 0, px < n_px - 1
    has_prev, has_next = py > 0, py < n_py - 1
    left = (shot, lax.rem(px + n_px - 1, n_px), py)
    right = (shot, lax.rem(px + 1, n_px), py)
    prev = (shot, px, lax.rem(py + n_py - 1, n_py))
    after_py = (shot, px, lax.rem(py + 1, n_py))
    mate = (shot + 1 - 2 * core, px, py)
    near1 = (shot + 2 * (1 - 2 * bit0), px, py)
    near2 = (shot + 4 * (1 - 2 * bit1), px, py)
    near3 = (shot + 2 * (1 - 2 * bit0) + 4 * (1 - 2 * bit1), px, py)
    near4 = (shot + 8 * (1 - 2 * bit2), px, py)

    inner = (slice(4, 4 + NZ), slice(8, 8 + ROWS), slice(None))
    load_now = pltpu.make_async_copy(now_h, fnow.at[inner], in_sem.at[0])
    load_adj = pltpu.make_async_copy(adj_h, adj, in_sem.at[1])
    load_speed = pltpu.make_async_copy(speed_h, speed, in_sem.at[2])
    load_before = pltpu.make_async_copy(before_h, before, in_sem.at[3])
    load_after = pltpu.make_async_copy(after_h, after, in_sem.at[4])
    load_small = [
        pltpu.make_async_copy(source, target, in_sem.at[5 + k])
        for k, (source, target) in enumerate(
            ((src_pos_h, src_pos), (src_amp_h, src_amp), (rec_pos_h, rec_pos), (observed_h, observed))
        )
    ]
    for load in (load_now, load_adj, load_speed, *load_small, load_before, load_after):
        load.start()

    barrier = pltpu.get_barrier_semaphore()
    partners = (left, right, prev, after_py, mate, near1, near2, near3, near4)
    for device in partners:
        pl.semaphore_signal(barrier, inc=1, device_id=device, device_id_type=MESH)

    lane = lax.broadcasted_iota(jnp.int32, (8, COLS), 1)
    group = lane // 4

    def remote(src, dst, sem, device):
        return pltpu.make_async_remote_copy(
            src_ref=src, dst_ref=dst, send_sem=send_sem.at[sem], recv_sem=recv_sem.at[sem],
            device_id=device, device_id_type=MESH,
        )

    class Halo:
        def __init__(self, k, field):
            low, high = slice(8, 12), slice(4 + ROWS, 8 + ROWS)
            over, under = slice(8 + ROWS, 12 + ROWS), slice(4, 8)
            depth = slice(4, 4 + NZ)
            self.to_left = remote(field.at[depth, low, :], field.at[depth, over, :], 4 * k, left)
            self.to_right = remote(field.at[depth, high, :], field.at[depth, under, :], 4 * k + 1, right)
            self.to_prev = remote(pack.at[2 * k], halo.at[2 * k + 1], 4 * k + 2, prev)
            self.to_next = remote(pack.at[2 * k + 1], halo.at[2 * k], 4 * k + 3, after_py)

        def send_left(self):
            pl.when(has_left)(self.to_left.start)

        def send_right(self):
            pl.when(has_right)(self.to_right.start)

        def send_lanes(self):
            pl.when(has_prev)(self.to_prev.start)
            pl.when(has_next)(self.to_next.start)

        def wait_left(self):
            pl.when(has_left)(self.to_right.wait_recv)

        def wait_right(self):
            pl.when(has_right)(self.to_left.wait_recv)

        def wait_lanes(self):
            pl.when(has_next)(self.to_prev.wait_recv)
            pl.when(has_prev)(self.to_next.wait_recv)

        drained = False

        def drain(self):
            if not self.drained:
                pl.when(has_left)(self.to_left.wait_send)
                pl.when(has_right)(self.to_right.wait_send)
            self.drained = True

        def finish(self):
            self.drain()
            pl.when(has_prev)(self.to_prev.wait_send)
            pl.when(has_next)(self.to_next.wait_send)

    halo_now, halo_cadj, halo_mid, halo_cmid = (
        Halo(k, field) for k, field in enumerate((fnow, cadj, fmid, cmid))
    )

    def packed(z, value, carry):
        to_prev, to_next = carry
        moved = pltpu.roll(value, lax.rem(4 * z + 4, COLS), 1)
        return (
            jnp.where(group == lax.rem(z + 1, NZ), moved, to_prev),
            jnp.where(group == z, moved, to_next),
        )

    def laplace(field, k, z, tile):
        row = 8 + 8 * tile
        centre = field[z + 4, row:row + 8, :]
        from_prev = pltpu.roll(halo[2 * k, 8 * tile:8 * tile + 8, :], COLS - 4 - 4 * z, 1)
        from_next = pltpu.roll(halo[2 * k + 1, 8 * tile:8 * tile + 8, :], COLS - 4 - 4 * z, 1)
        total = (3.0 * WEIGHTS[0]) * centre
        for r in range(1, 5):
            near = field[z + 4 + r, row:row + 8, :] + field[z + 4 - r, row:row + 8, :]
            near = near + field[z + 4, row + r:row + r + 8, :] + field[z + 4, row - r:row - r + 8, :]
            near = near + pltpu.roll(jnp.where(lane >= COLS - r, from_prev, centre), r, 1)
            near = near + pltpu.roll(jnp.where(lane < r, from_next, centre), COLS - r, 1)
            total = total + WEIGHTS[r] * near
        return centre, total

    zero = jnp.zeros((8, COLS), jnp.float32)

    def over_depth(tile, k, step):
        def body(z, carry):
            value = step(z)
            return packed(z, value, carry) if k is not None else carry
        carry = lax.fori_loop(0, NZ, body, (zero, zero) if k is not None else 0, unroll=UNROLL)
        if k is not None:
            pack[2 * k, 8 * tile:8 * tile + 8, :] = carry[0]
            pack[2 * k + 1, 8 * tile:8 * tile + 8, :] = carry[1]

    load_now.wait()
    pl.semaphore_wait(barrier, len(partners))
    halo_now.send_left()
    halo_now.send_right()

    for field in (fnow, fmid, cadj, cmid):
        for plane in (0, 1, 2, 3, NZ + 4, NZ + 5, NZ + 6, NZ + 7):
            field[plane] = jnp.zeros((ROWS + 16, COLS), jnp.float32)

    @pl.when(px == 0)
    def _():
        def body(z, _):
            for field in (fnow, fmid, cadj, cmid):
                field[z + 4, 0:8, :] = jnp.zeros((8, COLS), jnp.float32)
            return 0
        lax.fori_loop(0, NZ, body, 0)

    @pl.when(px == n_px - 1)
    def _():
        def body(z, _):
            for field in (fnow, fmid, cadj, cmid):
                field[z + 4, 8 + ROWS:16 + ROWS, :] = jnp.zeros((8, COLS), jnp.float32)
            return 0
        lax.fori_loop(0, NZ, body, 0)

    @pl.when(py == 0)
    def _():
        for k in range(4):
            halo[2 * k] = jnp.zeros((ROWS, COLS), jnp.float32)

    @pl.when(py == n_py - 1)
    def _():
        for k in range(4):
            halo[2 * k + 1] = jnp.zeros((ROWS, COLS), jnp.float32)

    for tile in range(TILES):
        over_depth(tile, 0, lambda z: fnow[z + 4, 8 + 8 * tile:16 + 8 * tile, :])
    halo_now.send_lanes()

    load_adj.wait()
    load_speed.wait()

    def coef_at(z, rows):
        value = speed[z, rows, :]
        return TIME_FACTOR * value * value

    for tile in range(TILES):
        rows, ext = slice(8 * tile, 8 * tile + 8), slice(8 + 8 * tile, 16 + 8 * tile)

        def scale(z):
            value = coef_at(z, rows) * adj[z, rows, :]
            cadj[z + 4, ext, :] = value
            return value

        over_depth(tile, 1, scale)
    halo_cadj.send_lanes()

    for load in load_small:
        load.wait()
    first_start, second_start = px * ROWS, py * COLS
    place = lax.broadcasted_iota(jnp.int32, (8, COLS), 0) * COLS + lane
    first, second = src_pos[1] - first_start, src_pos[2] - second_start
    owned = (first >= 0) & (first < ROWS) & (second >= 0) & (second < COLS)
    key = jnp.where(owned, (src_pos[0] * ROWS + first) * COLS + second, -1)

    def spread(row, j):
        return jnp.broadcast_to(row[:, j:j + 1], (8, COLS))

    spikes = [(spread(key, j), spread(src_amp[0:1, :], j), spread(src_amp[1:2, :], j)) for j in range(NSRC)]
    for tile in range(TILES):
        rows = slice(8 * tile, 8 * tile + 8)

        def sources(z, _):
            here = place + (z * ROWS + 8 * tile) * COLS
            one, two = zero, zero
            for cell, amp_one, amp_two in spikes:
                hit = here == cell
                one = one + jnp.where(hit, amp_one, 0.0)
                two = two + jnp.where(hit, amp_two, 0.0)
            s_one[z, rows, :] = one
            s_two[z, rows, :] = two
            return 0

        lax.fori_loop(0, NZ, sources, 0, unroll=4)

    first = rec_pos[1] - first_start
    inside = (first >= 0) & (first < ROWS)
    cell_row = jnp.where(inside, rec_pos[0] * ROWS + first, -1).astype(jnp.float32)
    second = (rec_pos[2] - second_start).astype(jnp.float32)
    data = jnp.transpose(jnp.concatenate([second, observed[...], jnp.zeros((5, NREC), jnp.float32)], axis=0))
    column = lax.broadcasted_iota(jnp.int32, (NREC, COLS), 1).astype(jnp.float32) == data[:, 0:1]
    parts = [column.astype(jnp.float32).astype(jnp.bfloat16)]
    for k in range(2):
        rest = jnp.where(column, jnp.broadcast_to(data[:, k + 1:k + 2], (NREC, COLS)), 0.0)
        for _ in range(3):
            part = rest.astype(jnp.bfloat16)
            rest = rest - part.astype(jnp.float32)
            parts.append(part)
    DEPTHS = 8

    def receivers(step, _):
        base = step * (DEPTHS * ROWS)
        index = lax.broadcasted_iota(jnp.int32, (DEPTHS * ROWS, NREC), 0) + base
        hot = (index.astype(jnp.float32) == cell_row).astype(jnp.float32).astype(jnp.bfloat16)
        sums = [jnp.dot(hot, part, preferred_element_type=jnp.float32) for part in parts]
        depths = pl.ds(step * DEPTHS, DEPTHS)
        count[depths] = sums[0].reshape(DEPTHS, ROWS, COLS)
        obs_two[depths] = (sums[1] + sums[2] + sums[3]).reshape(DEPTHS, ROWS, COLS)
        obs_three[depths] = (sums[4] + sums[5] + sums[6]).reshape(DEPTHS, ROWS, COLS)
        return 0

    lax.fori_loop(0, NZ // DEPTHS, receivers, 0)
    halo_now.drain()
    halo_cadj.send_left()
    halo_cadj.send_right()

    load_before.wait()
    halo_now.wait_lanes()

    def mid_tile(tile):
        rows, ext = slice(8 * tile, 8 * tile + 8), slice(8 + 8 * tile, 16 + 8 * tile)

        def step(z):
            centre, lap = laplace(fnow, 0, z, tile)
            lap1[z, rows, :] = lap
            value = 2.0 * centre - before[z, rows, :] + coef_at(z, rows) * lap + s_one[z, rows, :]
            fmid[z + 4, ext, :] = value
            mid[z, rows, :] = value
            return value

        over_depth(tile, 2, step)

    mid_tile(1)
    halo_now.wait_left()
    mid_tile(0)
    halo_mid.send_left()
    halo_now.wait_right()
    mid_tile(2)
    halo_mid.send_right()
    halo_mid.send_lanes()

    load_after.wait()
    halo_cadj.wait_lanes()

    def base_tile(tile):
        rows = slice(8 * tile, 8 * tile + 8)

        def step(z):
            _, lap = laplace(cadj, 1, z, tile)
            amid[z, rows, :] = 2.0 * adj[z, rows, :] - after[z, rows, :] + lap - obs_three[z, rows, :]

        over_depth(tile, None, step)

    base_tile(1)
    halo_cadj.wait_left()
    base_tile(0)
    halo_cadj.wait_right()
    base_tile(2)

    halo_mid.wait_lanes()

    def last_tile(tile):
        rows, ext = slice(8 * tile, 8 * tile + 8), slice(8 + 8 * tile, 16 + 8 * tile)

        def step(z):
            centre, lap = laplace(fmid, 2, z, tile)
            velocity = speed[z, rows, :]
            coef = TIME_FACTOR * velocity * velocity
            value = 2.0 * centre - fnow[z + 4, ext, :] + coef * lap + s_two[z, rows, :]
            last[z, rows, :] = value
            adjoint = amid[z, rows, :] + count[z, rows, :] * value
            amid[z, rows, :] = adjoint
            image = adjoint * lap1[z, rows, :] + adj[z, rows, :] * lap
            owner = z // 2
            term[owner // 8, lax.rem(owner // 4, 2), lax.rem(owner // 2, 2), lax.rem(owner, 2), lax.rem(z, 2), rows, :] = (
                2.0 * TIME_FACTOR * velocity * image
            )
            scaled = coef * adjoint
            cmid[z + 4, ext, :] = scaled
            return scaled

        over_depth(tile, 3, step)

    last_tile(1)
    halo_mid.wait_left()
    last_tile(0)
    halo_cmid.send_left()
    halo_mid.wait_right()
    last_tile(2)
    sum_a = remote(term.at[:, :, :, 1 - core], ra, SUM_A, mate)
    sum_a.start()
    halo_cmid.send_right()
    halo_cmid.send_lanes()

    sum_a.wait_recv()

    def add_a(step, _):
        i, j = step // 2, lax.rem(step, 2)
        for k in range(2):
            sa[i, j, k] = term[i, j, k, core] + ra[i, j, k]
        return 0

    lax.fori_loop(0, 4, add_a, 0)
    others = ((3, near3, 1 - bit1, 1 - bit0), (2, near2, 1 - bit1, bit0), (1, near1, bit1, 1 - bit0))
    sums = [remote(sa.at[:, i, j], rb.at[k - 1], SUM_B + k, device) for k, device, i, j in others]
    for copy in sums:
        copy.start()

    def adj_tile(tile):
        rows = slice(8 * tile, 8 * tile + 8)
        ext = slice(8 + 8 * tile, 16 + 8 * tile)

        def step(z):
            _, lap = laplace(cmid, 3, z, tile)
            alast[z, rows, :] = (
                2.0 * amid[z, rows, :] - adj[z, rows, :] + lap
                + (count[z, rows, :] * fmid[z + 4, ext, :] - obs_two[z, rows, :])
            )

        over_depth(tile, None, step)

    halo_cmid.wait_lanes()
    adj_tile(1)

    for copy in sums:
        copy.wait_recv()
    for i in range(2):
        sc[i] = sa[i, bit1, bit0] + rb[0, i] + rb[1, i] + rb[2, i]
    sum_d = remote(sc, rd, SUM_D, near4)
    sum_d.start()
    sum_d.wait_recv()
    for i in range(2):
        new[i, bit1, bit0, core] = speed[pl.ds(16 * i + 2 * lax.rem(shot, 8), 2)] - rate[0] * (sc[i] + rd[i])

    own = new.at[:, bit1, bit0, core]
    gathers = [remote(own, own, ALL_B + k, device) for k, device, _, _ in others]
    for copy in gathers:
        copy.start()
    grad[...] = sc[bit2] + rd[bit2]
    halo_cmid.wait_left()
    adj_tile(0)
    halo_cmid.wait_right()
    adj_tile(2)
    for copy in gathers:
        copy.wait_recv()
    own = new.at[:, :, :, core]
    all_a = remote(own, own, ALL_A, mate)
    all_a.start()


    all_a.wait_recv()

    for field in (halo_now, halo_cadj, halo_mid, halo_cmid):
        field.finish()
    for copy in (sum_a, *sums, sum_d, *gathers, all_a):
        copy.wait_send()


def write(*refs):
    sem = refs[12]
    copies = [pltpu.make_async_copy(refs[k], refs[6 + k], sem.at[k]) for k in range(6)]
    for copy in copies:
        copy.start()
    for copy in copies:
        copy.wait()


def local(before, now, after, adj, speed, src_pos, src_amp, rec_pos, observed, rate):
    f32 = jnp.float32
    block = (NZ, ROWS, COLS)
    padded = (NZ + 8, ROWS + 16, COLS)
    slab = (2, ROWS, COLS)

    def vmem(*shape):
        return pltpu.VMEM(shape, f32)

    in_hbm = pl.BlockSpec(memory_space=pltpu.HBM)
    in_vmem = pl.BlockSpec(memory_space=pltpu.VMEM)
    in_smem = pl.BlockSpec(memory_space=pltpu.SMEM)
    outs = pl.pallas_call(
        kernel,
        out_shape=[jax.ShapeDtypeStruct(block, f32)] * 4
        + [jax.ShapeDtypeStruct((2, 2, 2, 2) + slab, f32), jax.ShapeDtypeStruct(slab, f32)],
        in_specs=[in_hbm] * 9 + [in_smem],
        out_specs=[in_vmem] * 6,
        scratch_shapes=[vmem(*padded)] * 4
        + [vmem(*block)] * 5
        + [
            pltpu.VMEM((3, 1, NSRC), jnp.int32), vmem(2, NSRC),
            pltpu.VMEM((3, 1, NREC), jnp.int32), vmem(2, NREC),
        ]
        + [vmem(*block)] * 5
        + [vmem(8, ROWS, COLS)] * 2
        + [
            vmem(2, 2, 2, 2, *slab),
            vmem(2, 2, 2, *slab), vmem(2, 2, 2, *slab),
            vmem(3, 2, *slab),
            vmem(2, *slab), vmem(2, *slab),
        ]
        + [
            pltpu.SemaphoreType.DMA((9,)),
            pltpu.SemaphoreType.DMA((N_SEMS,)),
            pltpu.SemaphoreType.DMA((N_SEMS,)),
        ],
        compiler_params=pltpu.CompilerParams(
            collective_id=0, has_side_effects=True, vmem_limit_bytes=53100 * 1024
        ),
        name="window",
    )(
        before[0], now[0], after[0], adj[0], speed,
        src_pos.transpose(2, 0, 1), src_amp[0], rec_pos.transpose(2, 0, 1), observed[0], rate,
    )
    mid, last, adj_mid, adj_last, new, grad = pl.pallas_call(
        write,
        out_shape=[jax.ShapeDtypeStruct(out.shape, f32) for out in outs],
        in_specs=[in_vmem] * 6,
        out_specs=[in_hbm] * 6,
        scratch_shapes=[pltpu.SemaphoreType.DMA((6,))],
        compiler_params=pltpu.CompilerParams(vmem_limit_bytes=1024 * 1024),
        name="write",
    )(*outs)
    return mid[None], last[None], adj_mid[None], adj_last[None], new.reshape(block), grad


def solution(mesh):
    wave = P("shot", None, "px", "py")
    group = P("shot", None, None)
    return jax.shard_map(
        local,
        mesh=mesh,
        in_specs=(wave, wave, wave, wave, P(None, "px", "py"), group, group, group, group, P()),
        out_specs=(wave, wave, wave, wave, P(None, "px", "py"), P("shot", "px", "py")),
        check_vma=False,
    )
```
